32 devices in a mesh: groups: 2 (over y), seq: 4 (over z), mp: 2 (over x), rep: 2 (over core).
Axes of the slice: x: 2, y: 2, z: 4, core: 2. Of those that a mesh axis runs over, the one named last changes fastest.
Arguments:
- grad_hidden: bfloat16 [240, 24576], P(('groups', 'mp', 'rep'), 'seq'), parts along dimension 0, may hold values from -6 to 6
- w_up: bfloat16 [8192, 24576], P(('mp', 'rep'), 'seq'), may hold values from -0.0390625 to 0.0390625
- pool_a: bfloat16 [8, 8192, 64], P(('groups', 'seq'), ('mp', 'rep')), parts along dimension 0, may hold values from -0.75 to 0.75
- pool_b: bfloat16 [8, 64, 24576], P(('groups', 'seq')), parts along dimension 0, may hold values from -0.0390625 to 0.0390625
- seg_adapter: int32 [8, 2], P('groups'), parts along dimension 0, may hold values from 0 to 3
- adapter_slot: int32 [8], P('groups'), parts along dimension 0, may hold values from 0 to 3, each once
- seg_len: int32 [8, 2], P('groups'), parts along dimension 0, may hold values from 1 to 15, as said below
Outputs:
- input_grad: bfloat16 [240, 8192], P(('groups', 'seq'), ('mp', 'rep')), parts along dimension 0
The draws below stay inside these ranges and needn't reach their ends.
There are 2 independent parts, one for each index of `groups`. The reference program is written for one: setup_inputs(seed, part) draws one part's arguments, and reference() takes and returns one part's arrays. A program takes and returns all parts, laid end to end along the dimension named above; an argument that names none is the same for every part. Nothing has to cross between parts.
Inputs may be any that keep to these rules, and one draw needn't show every extreme that they name: `adapter_slot`: pool slot of every adapter, each slot once; slot q is held by the pool shard q. `seg_len`: valid tokens stand first in their segment.
All inputs are finite; a program needn't handle non-finite values.
Results may differ from the reference program's by a relative error of at most 0.0029.
Values may be sent and summed in bfloat16 or wider, within the bound.
A program may use at most 128 MiB of HBM per device.

```python
import math
import jax
import jax.numpy as jnp
import numpy as np

D = 8192
FW = 24576
R = 64
TOK_DEV = 30
SEGS_BLK = 2
SEG = 15
BLOCKS = 4
TOKENS = 120
ADAPTERS = 4


def draw_seg_len(key, part):
    key = jax.random.fold_in(key, 11)
    first_key, second_key, third_key = jax.random.split(key, 3)
    total = BLOCKS * SEGS_BLK
    lengths = jax.random.randint(first_key, (BLOCKS, SEGS_BLK), 1, SEG + 1)
    chosen = jax.random.randint(second_key, (), 0, total)
    other = (chosen + 1 + jax.random.randint(third_key, (), 0, total - 1)) % total
    flat_index = jnp.arange(total, dtype=jnp.int32).reshape(BLOCKS, SEGS_BLK)
    lengths = jnp.where(flat_index == chosen, SEG, lengths)
    lengths = jnp.where(flat_index == other, 1, lengths)
    return lengths.astype(jnp.int32)


def with_ends(values, rng, smallest, high):
    longest = values.shape.index(max(values.shape))
    spots = []
    for shift in (0, 1):
        where = [jax.random.randint(jax.random.fold_in(rng, axis), (), 0, length) for axis, length in enumerate(values.shape)]
        where[longest] = (where[longest] + shift) % values.shape[longest]
        spots.append(tuple(where))
    return values.at[spots[0]].set(smallest).at[spots[1]].set(high)


def strengthened(result, rng, source, target, shards_of, factor):
    owner, partner = [(jnp.arange(result.shape[axis_at]) // (result.shape[axis_at] // shards_of)).reshape([-1 if axis == axis_at else 1 for axis in range(result.ndim)]) for axis_at in (source, target)]
    chosen = jax.random.permutation(rng, shards_of)[partner]
    strong = (owner == chosen) | (owner == (partner + shards_of // 2) % shards_of)
    return jnp.where(strong, factor * result, result)


def block_scale(key, dims, cuts, least, top_value):
    loudness, own = 1.0, jax.random.fold_in(key, 6)
    for dim, shards_of in cuts:
        draws = jnp.exp(jax.random.uniform(jax.random.fold_in(own, dim), (shards_of,), jnp.float32, least / len(cuts), top_value / len(cuts)))
        loudness = loudness * jnp.repeat(draws, dims[dim] // shards_of).reshape([-1 if axis == dim else 1 for axis in range(len(dims))])
    return loudness


def rank_bounds(number_of, slope):
    loads = [(1 << 20) // math.isqrt(standing ** slope) + 1 for standing in range(1, number_of + 1)]
    scale = 1 + sum(loads) // (1 << 30)
    return np.cumsum(np.array([max(1, weight // scale) for weight in loads]))


def ranked(rng, shape, count, slope):
    listing = rank_bounds(count, slope)
    ticket = jax.random.randint(jax.random.fold_in(rng, 1), shape, 0, int(listing[count - 1]))
    rank = jnp.searchsorted(jnp.asarray(listing, jnp.int32), ticket, side="right")
    return jax.random.permutation(jax.random.fold_in(rng, 2), count)[rank].astype(jnp.int32)


def gaussian(stream_key, shape, width, bound, shards=(), kind=jnp.bfloat16):
    loudness = block_scale(stream_key, shape, shards, -0.22, 0.18) if shards else 1.0
    drawn = jax.random.normal(stream_key, shape, jnp.float32) * width * loudness
    return jnp.minimum(jnp.maximum(drawn, -bound), bound).astype(kind)


def gaussian_with(rng, shape, scale, bound, cuts, heavy, held_as=jnp.bfloat16):
    drawn = scale * jax.random.normal(rng, shape, jnp.float32)
    if cuts:
        drawn = drawn * block_scale(rng, shape, cuts, -0.22, 0.18)
    return jnp.clip(strengthened(drawn, jax.random.fold_in(rng, 3), *heavy), -bound, bound).astype(held_as)


def setup_inputs(seed: int = 0, part: int = 0) -> dict:
    seeds = jax.random.split(jax.random.key(seed), 8)
    part_keys = jax.random.split(jax.random.fold_in(seeds[7], part), 8)
    return {
        "grad_hidden": gaussian_with(part_keys[0], (TOKENS, FW), 1.0, 6.0, ((0, 4), (1, 4)), (1, 0, 4, 2.0)),
        "w_up": gaussian(seeds[1], (D, FW), FW ** -0.5, 0.0390625, ((0, 4), (1, 4))),
        "pool_a": gaussian(part_keys[2], (ADAPTERS, D, R), R ** -0.5, 0.75, ((0, 4), (1, 4))),
        "pool_b": gaussian(part_keys[3], (ADAPTERS, R, FW), FW ** -0.5, 0.0390625, ((0, 4),)),
        "seg_adapter": with_ends(ranked(part_keys[4], (BLOCKS, SEGS_BLK), ADAPTERS, 2), jax.random.fold_in(part_keys[4], 3), 0, ADAPTERS - 1).astype(jnp.int32),
        "adapter_slot": jax.random.permutation(part_keys[5], ADAPTERS).astype(jnp.int32),
        "seg_len": draw_seg_len(jax.random.fold_in(jax.random.fold_in(seeds[7], part), 71), part),
    }


adapter_scale_factor = 0.5


def reference(grad_hidden, w_up, pool_a, pool_b, seg_adapter, adapter_slot, seg_len):
    slot_ids = adapter_slot[seg_adapter].astype(jnp.int32)
    position = jnp.arange(TOK_DEV, dtype=jnp.int32)
    within = position % SEG
    length_tok = jnp.repeat(seg_len, SEG, axis=1)
    valid = (within[None, :] < length_tok).reshape(-1)
    masked = jnp.where(valid[:, None], grad_hidden, jnp.zeros_like(grad_hidden))
    flat_slots = slot_ids.reshape(-1)
    segments = BLOCKS * SEGS_BLK
    segment_row_count = masked.reshape(segments, SEG, FW).astype(jnp.float32)
    selected_up_factor = pool_b[flat_slots].astype(jnp.float32)
    adapter_rank_width = (adapter_scale_factor * jnp.einsum("ezu,egu->ezg", segment_row_count, selected_up_factor)).astype(jnp.bfloat16)
    chosen_a = pool_a[flat_slots].astype(jnp.float32)
    low_term = jnp.einsum("nsr,ndr->nsd", adapter_rank_width.astype(jnp.float32), chosen_a).reshape(TOKENS, D)
    frozen_term = jnp.dot(masked, w_up.T, preferred_element_type=jnp.float32)
    return (frozen_term + low_term).astype(jnp.bfloat16)
```

```python
import functools

import jax
import jax.numpy as jnp
from jax import lax
from jax.experimental import pallas as pl
from jax.experimental.pallas import tpu as pltpu
from jax.sharding import PartitionSpec as P

R = 64
TOK_DEV = 30
SEG = 15
PAD = 32
K_CHUNKS = 2
D_TILE = 256
MESH = pl.DeviceIdType.MESH

adapter_scale_factor = 0.5
NT = (((1,), (1,)), ((), ()))


def flip(index, bits):
    result, bit = index, 1
    while bit <= bits:
        if bits & bit:
            result = result + bit - 2 * bit * ((index // bit) % 2)
        bit *= 2
    return result


def kernel(
    ns, nmp, nrep,
    grad_hbm, w_hbm, a_hbm, b_hbm, adapter_ref, slot_ref, len_ref,
    out_ref,
    own_raw, g, w, a, b, acc, low_own, low_in, low_all, low_rows, quant_out, quant_in, scale_out, scale_in,
    own_sem, w_sem, a_sem, b_own_sem,
    gx_send, gx_recv, gs_send, gs_recv, b_send, b_recv,
    l_send, l_recv, m_send, m_recv, q_send, q_recv, c_send, c_recv,
):
    z, x, c = lax.axis_index("seq"), lax.axis_index("mp"), lax.axis_index("rep")
    members = nmp * nrep
    me = x * nrep + c
    blocks = ns
    per_dev = blocks // members
    rank_part = b.shape[1]
    hidden = w.shape[1]
    chunk = hidden // K_CHUNKS
    d_part = w.shape[0]
    tokens = blocks * PAD
    z_order = list(range(ns - 1, 0, -1))
    if ns == 4:
        z_order = [2, 3, 1]

    own_copy = pltpu.make_async_copy(grad_hbm, own_raw, own_sem)
    own_copy.start()

    barrier = pltpu.get_barrier_semaphore()
    for s in z_order:
        pl.semaphore_signal(barrier, inc=1, device_id={"seq": flip(z, s)}, device_id_type=MESH)
    for s in range(1, members):
        peer = flip(me, s)
        pl.semaphore_signal(
            barrier, inc=1, device_id={"mp": peer // nrep, "rep": peer % nrep}, device_id_type=MESH
        )

    def w_copy(t):
        rows = pl.ds(pl.multiple_of(t * D_TILE, D_TILE), D_TILE)
        return pltpu.make_async_copy(w_hbm.at[rows], w.at[rows], w_sem.at[t])

    tiles = d_part // D_TILE
    for t in range(tiles):
        w_copy(t).start()
    a_copy = pltpu.make_async_copy(a_hbm.at[0], a, a_sem)
    a_copy.start()

    own_copy.wait()
    row = lax.broadcasted_iota(jnp.int32, (TOK_DEV, 1), 0)
    second = row >= SEG
    for i in range(per_dev):
        block = me * per_dev + i
        length = jnp.where(second, len_ref[block, 1] + SEG, len_ref[block, 0])
        rows = own_raw[i * TOK_DEV:(i + 1) * TOK_DEV, :]
        rows = jnp.where(row < length, rows.astype(jnp.float32), 0.0).astype(jnp.bfloat16)
        rows = jnp.concatenate([rows, jnp.zeros((PAD - TOK_DEV, hidden), jnp.bfloat16)], axis=0)
        g[me, i] = rows

    pl.semaphore_wait(barrier, ns - 1 + members - 1)

    def b_part(q):
        return b_hbm.at[0, pl.ds(pl.multiple_of(me * rank_part, rank_part), rank_part),
                        pl.ds(pl.multiple_of(q * hidden, hidden), hidden)]

    b_copies = {}
    for s in z_order:
        b_copies[s] = pltpu.make_async_remote_copy(
            src_ref=b_part(flip(z, s)), dst_ref=b.at[s],
            send_sem=b_send.at[s], recv_sem=b_recv.at[s],
            device_id={"seq": flip(z, s)}, device_id_type=MESH)

    def g_part(member, k):
        return g.at[member, :, :, k * chunk:(k + 1) * chunk]

    def g_copy(member, k, send, recv, s, device):
        return pltpu.make_async_remote_copy(
            src_ref=g_part(member, k), dst_ref=g_part(member, k),
            send_sem=send.at[s, k], recv_sem=recv.at[s, k],
            device_id=device, device_id_type=MESH)

    across, beside = {}, {}
    sibling = {"rep": flip(c, 1)}
    for k in range(K_CHUNKS):
        for s in range(1, nmp):
            across[s, k] = g_copy(me, k, gx_send, gx_recv, s, {"mp": flip(x, s)})
            across[s, k].start()
        if k == 0:
            for s in z_order:
                b_copies[s].start()
        beside[0, k] = g_copy(me, k, gs_send, gs_recv, 0, sibling)
        beside[0, k].start()
    b_own = pltpu.make_async_copy(b_part(z), b.at[0], b_own_sem)
    b_own.start()

    for k in range(K_CHUNKS):
        for s in range(1, nmp):
            across[s, k].wait_recv()
            beside[s, k] = g_copy(flip(x, s) * nrep + c, k, gs_send, gs_recv, s, sibling)
            beside[s, k].start()
        for s in range(nmp):
            beside[s, k].wait_recv()

        def tile_step(t, carry, k=k):
            rows = pl.ds(pl.multiple_of(t * D_TILE, D_TILE), D_TILE)
            if k == 0:
                w_copy(t).wait()
            part = lax.dot_general(
                g[:, :, :, k * chunk:(k + 1) * chunk].reshape(tokens, chunk),
                w[rows, k * chunk:(k + 1) * chunk], NT,
                preferred_element_type=jnp.float32)
            if k == 0:
                acc[:, rows] = part
            else:
                acc[:, rows] += part
            return carry

        lax.fori_loop(0, tiles, tile_step, 0)

    lane = lax.broadcasted_iota(jnp.int32, (1, tokens), 1)
    slots = jnp.zeros((1, tokens), jnp.int32)
    for block in range(blocks):
        for j in range(2):
            slot = slot_ref[adapter_ref[block, j]]
            slots = jnp.where(lane >= block * PAD + j * SEG, slot, slots)

    masked = g[...].reshape(tokens, hidden)
    picked = jnp.zeros((rank_part, tokens), jnp.float32)
    for s in [0] + z_order[::-1]:
        if s == 0:
            b_own.wait()
        else:
            b_copies[s].wait_recv()
        every = lax.dot_general(b[s], masked, NT, preferred_element_type=jnp.float32)
        picked = jnp.where(slots == flip(z, s), every, picked)
    low_own[...] = picked

    low_copies = []
    for s in z_order:
        low_copies.append(pltpu.make_async_remote_copy(
            src_ref=low_own, dst_ref=low_in.at[s], send_sem=l_send.at[s], recv_sem=l_recv.at[s],
            device_id={"seq": flip(z, s)}, device_id_type=MESH))
        low_copies[-1].start()
    total = picked
    for s, copy in zip(z_order, low_copies):
        copy.wait_recv()
        total = total + low_in[s]
    low_all[me] = (adapter_scale_factor * total).astype(jnp.bfloat16)

    member_copies = []
    for s in range(members - 1, 0, -1):
        peer = flip(me, s)
        member_copies.append(pltpu.make_async_remote_copy(
            src_ref=low_all.at[me], dst_ref=low_all.at[me], send_sem=m_send.at[s], recv_sem=m_recv.at[s],
            device_id={"mp": peer // nrep, "rep": peer % nrep}, device_id_type=MESH))
        member_copies[-1].start()
    for copy in member_copies:
        copy.wait_recv()
    a_copy.wait()

    low_t = low_all[...].astype(jnp.float32).reshape(members * rank_part, tokens)
    low_t = jnp.where(slots == z, low_t, 0.0)
    low_rows[...] = low_t.T.astype(jnp.bfloat16)

    def block_sum(block):
        rows = pl.ds(pl.multiple_of(block * PAD, PAD), PAD)
        low_term = lax.dot_general(low_rows[rows, :], a[...], NT, preferred_element_type=jnp.float32)
        return acc[rows, :] + low_term

    groups = d_part // 128
    out_copies = []
    for s in z_order:
        dest = flip(z, s)
        value = block_sum(dest)
        largest = jnp.abs(value[:, :128])
        for i in range(1, groups):
            largest = jnp.maximum(largest, jnp.abs(value[:, i * 128:(i + 1) * 128]))
        largest = jnp.max(largest.reshape(PAD // 8, 8, 128), axis=0)
        largest = jnp.maximum(largest, 1e-33)
        scale_out[s] = largest * (1.0 / 32767.0)
        inverse = jnp.tile(32767.0 / largest, (PAD // 8, 1))
        for i in range(groups):
            q = jnp.round(value[:, i * 128:(i + 1) * 128] * inverse)
            quant_out[s, :, i * 128:(i + 1) * 128] = q.astype(jnp.int32).astype(jnp.int16)
        for src, dst, send, recv in ((quant_out, quant_in, q_send, q_recv), (scale_out, scale_in, c_send, c_recv)):
            copy = pltpu.make_async_remote_copy(
                src_ref=src.at[s], dst_ref=dst.at[s], send_sem=send.at[s], recv_sem=recv.at[s],
                device_id={"seq": dest}, device_id_type=MESH)
            copy.start()
            out_copies.append(copy)

    rows = pl.ds(pl.multiple_of(z * PAD, PAD), PAD)
    acc[rows, :] = block_sum(z)
    for copy in out_copies:
        copy.wait_recv()
    scales = {s: jnp.tile(scale_in[s], (PAD // 8, 1)) for s in z_order}
    for i in range(groups):
        columns = slice(i * 128, (i + 1) * 128)
        result = acc[rows, columns]
        for s in z_order:
            result = result + quant_in[s, :, columns].astype(jnp.int32).astype(jnp.float32) * scales[s]
        out_ref[:, columns] = result[:TOK_DEV].astype(jnp.bfloat16)

    for copy in [*b_copies.values(), *across.values(), *beside.values(), *low_copies, *member_copies, *out_copies]:
        copy.wait_send()


def on_device(ns, nmp, nrep, grad_hidden, w_up, pool_a, pool_b, seg_adapter, adapter_slot, seg_len):
    members = nmp * nrep
    d_part, hidden = w_up.shape
    rank_part = R // members
    tokens = ns * PAD
    hbm = pl.BlockSpec(memory_space=pl.ANY)
    smem = pl.BlockSpec(memory_space=pltpu.SMEM)
    dma = pltpu.SemaphoreType.DMA
    bf16, f32 = jnp.bfloat16, jnp.float32
    scratch = [
        pltpu.VMEM(grad_hidden.shape, bf16),
        pltpu.VMEM((members, ns // members, PAD, hidden), bf16),
        pltpu.VMEM(w_up.shape, bf16),
        pltpu.VMEM((d_part, R), bf16),
        pltpu.VMEM((ns, rank_part, hidden), bf16),
        pltpu.VMEM((tokens, d_part), f32),
        pltpu.VMEM((rank_part, tokens), f32),
        pltpu.VMEM((ns, rank_part, tokens), f32),
        pltpu.VMEM((members, rank_part, tokens), bf16),
        pltpu.VMEM((tokens, R), bf16),
        pltpu.VMEM((ns, PAD, d_part), jnp.int16),
        pltpu.VMEM((ns, PAD, d_part), jnp.int16),
        pltpu.VMEM((ns, 8, 128), f32),
        pltpu.VMEM((ns, 8, 128), f32),
        dma, dma((d_part // D_TILE,)), dma, dma,
        dma((nmp, K_CHUNKS)), dma((nmp, K_CHUNKS)), dma((nmp, K_CHUNKS)), dma((nmp, K_CHUNKS)),
        dma((ns,)), dma((ns,)),
        dma((ns,)), dma((ns,)), dma((members,)), dma((members,)),
        dma((ns,)), dma((ns,)), dma((ns,)), dma((ns,)),
    ]
    return pl.pallas_call(
        functools.partial(kernel, ns, nmp, nrep),
        out_shape=jax.ShapeDtypeStruct((TOK_DEV, d_part), bf16),
        in_specs=[hbm] * 4 + [smem] * 3,
        out_specs=pl.BlockSpec(memory_space=pltpu.VMEM),
        scratch_shapes=scratch,
        compiler_params=pltpu.CompilerParams(
            collective_id=0, has_side_effects=True, vmem_limit_bytes=56 * 1024 * 1024
        ),
        cost_estimate=pl.CostEstimate(
            flops=2 * tokens * d_part * hidden, bytes_accessed=2 * d_part * hidden, transcendentals=0
        ),
    )(grad_hidden, w_up, pool_a, pool_b, seg_adapter, adapter_slot, seg_len)


def solution(mesh):
    ns, nmp, nrep = mesh.shape["seq"], mesh.shape["mp"], mesh.shape["rep"]
    in_specs = (
        P(("groups", "mp", "rep"), "seq"),
        P(("mp", "rep"), "seq"),
        P(("groups", "seq"), ("mp", "rep"), None),
        P(("groups", "seq"), None, None),
        P("groups", None),
        P("groups"),
        P("groups", None),
    )
    out_specs = P(("groups", "seq"), ("mp", "rep"))
    return jax.shard_map(
        functools.partial(on_device, ns, nmp, nrep),
        mesh=mesh, in_specs=in_specs, out_specs=out_specs, check_vma=False,
    )
```

```python
import functools

import jax
import jax.numpy as jnp
from jax import lax
from jax.experimental import pallas as pl
from jax.experimental.pallas import tpu as pltpu
from jax.sharding import PartitionSpec as P

R = 64
TOK_DEV = 30
SEG = 15
PAD = 32
K_CHUNKS = 2
D_TILE = 256
MESH = pl.DeviceIdType.MESH

adapter_scale_factor = 0.5
NT = (((1,), (1,)), ((), ()))


def flip(index, bits):
    result, bit = index, 1
    while bit <= bits:
        if bits & bit:
            result = result + bit - 2 * bit * ((index // bit) % 2)
        bit *= 2
    return result


def kernel(
    ns, nmp, nrep,
    grad_hbm, w_hbm, a_hbm, b_hbm, adapter_ref, slot_ref, len_ref,
    out_ref,
    own_raw, g, w, a, b, acc, low_out, low_in, low_all, low_rows, quant_out, quant_in, scale_out, scale_in,
    own_sem, w_sem, a_sem, b_own_sem,
    gx_send, gx_recv, gs_send, gs_recv, b_send, b_recv,
    l_send, l_recv, m_send, m_recv, q_send, q_recv, c_send, c_recv,
):
    z, x, c = lax.axis_index("seq"), lax.axis_index("mp"), lax.axis_index("rep")
    members = nmp * nrep
    me = x * nrep + c
    blocks = ns
    per_dev = blocks // members
    rank_part = b.shape[1]
    hidden = w.shape[1]
    chunk = hidden // K_CHUNKS
    d_part = w.shape[0]
    tokens = blocks * PAD
    z_order = list(range(ns - 1, 0, -1))
    if ns == 4:
        z_order = [2, 3, 1]

    own_copy = pltpu.make_async_copy(grad_hbm, own_raw, own_sem)
    own_copy.start()

    barrier = pltpu.get_barrier_semaphore()
    for s in z_order:
        pl.semaphore_signal(barrier, inc=1, device_id={"seq": flip(z, s)}, device_id_type=MESH)
    for s in range(1, members):
        peer = flip(me, s)
        pl.semaphore_signal(
            barrier, inc=1, device_id={"mp": peer // nrep, "rep": peer % nrep}, device_id_type=MESH
        )

    def w_copy(t):
        rows = pl.ds(pl.multiple_of(t * D_TILE, D_TILE), D_TILE)
        return pltpu.make_async_copy(w_hbm.at[rows], w.at[rows], w_sem.at[t])

    tiles = d_part // D_TILE
    a_copy = pltpu.make_async_copy(a_hbm.at[0], a, a_sem)

    pl.semaphore_wait(barrier, ns - 1 + members - 1)

    def b_part(q):
        return b_hbm.at[0, pl.ds(pl.multiple_of(me * rank_part, rank_part), rank_part),
                        pl.ds(pl.multiple_of(q * hidden, hidden), hidden)]

    b_copies = {}
    for s in z_order:
        b_copies[s] = pltpu.make_async_remote_copy(
            src_ref=b_part(flip(z, s)), dst_ref=b.at[s],
            send_sem=b_send.at[s], recv_sem=b_recv.at[s],
            device_id={"seq": flip(z, s)}, device_id_type=MESH)
        b_copies[s].start()

    own_copy.wait()
    row = lax.broadcasted_iota(jnp.int32, (TOK_DEV, 1), 0)
    second = row >= SEG
    for i in range(per_dev):
        block = me * per_dev + i
        length = jnp.where(second, len_ref[1, block] + SEG, len_ref[0, block])
        rows = own_raw[i * TOK_DEV:(i + 1) * TOK_DEV, :]
        rows = jnp.where(row < length, rows.astype(jnp.float32), 0.0).astype(jnp.bfloat16)
        rows = jnp.concatenate([rows, jnp.zeros((PAD - TOK_DEV, hidden), jnp.bfloat16)], axis=0)
        g[me, i] = rows

    def g_part(member, k):
        return g.at[member, :, :, k * chunk:(k + 1) * chunk]

    def g_copy(member, k, send, recv, s, device):
        return pltpu.make_async_remote_copy(
            src_ref=g_part(member, k), dst_ref=g_part(member, k),
            send_sem=send.at[s, k], recv_sem=recv.at[s, k],
            device_id=device, device_id_type=MESH)

    across, beside = {}, {}
    sibling = {"rep": flip(c, 1)}
    for k in range(K_CHUNKS):
        for s in range(1, nmp):
            across[s, k] = g_copy(me, k, gx_send, gx_recv, s, {"mp": flip(x, s)})
            across[s, k].start()
        beside[0, k] = g_copy(me, k, gs_send, gs_recv, 0, sibling)
        beside[0, k].start()
    b_own = pltpu.make_async_copy(b_part(z), b.at[0], b_own_sem)
    b_own.start()
    for t in range(tiles):
        w_copy(t).start()
    a_copy.start()

    def frozen(k, first, last):
        def tile_step(t, carry):
            rows = pl.ds(pl.multiple_of(t * D_TILE, D_TILE), D_TILE)
            if k == 0:
                w_copy(t).wait()
            part = lax.dot_general(
                g[:, :, :, k * chunk:(k + 1) * chunk].reshape(tokens, chunk),
                w[rows, k * chunk:(k + 1) * chunk], NT,
                preferred_element_type=jnp.float32)
            if k == 0:
                acc[:, rows] = part
            else:
                acc[:, rows] += part
            return carry

        lax.fori_loop(first, last, tile_step, 0)

    for k in range(K_CHUNKS):
        for s in range(1, nmp):
            across[s, k].wait_recv()
            beside[s, k] = g_copy(flip(x, s) * nrep + c, k, gs_send, gs_recv, s, sibling)
            beside[s, k].start()
        for s in range(nmp):
            beside[s, k].wait_recv()
        if k < K_CHUNKS - 1:
            frozen(k, 0, tiles)

    lane = lax.broadcasted_iota(jnp.int32, (1, tokens), 1)
    slots = jnp.zeros((1, tokens), jnp.int32)
    for block in range(blocks):
        for j in range(2):
            slot = slot_ref[adapter_ref[j, block]]
            slots = jnp.where(lane >= block * PAD + j * SEG, slot, slots)

    def low_part(s):
        every = lax.dot_general(
            b[s], g[...].reshape(tokens, hidden), NT, preferred_element_type=jnp.float32)
        return jnp.where(slots == flip(z, s), every, 0.0)

    b_own.wait()
    total = low_part(0)
    last = K_CHUNKS - 1
    low_copies = []
    for s in range(1, ns):
        if s == min(2, ns - 1):
            frozen(last, 0, tiles // 2)
        b_copies[s].wait_recv()
        low_out[s] = low_part(s)
        low_copies.append(pltpu.make_async_remote_copy(
            src_ref=low_out.at[s], dst_ref=low_in.at[s], send_sem=l_send.at[s], recv_sem=l_recv.at[s],
            device_id={"seq": flip(z, s)}, device_id_type=MESH))
        low_copies[-1].start()
    frozen(last, tiles // 2, tiles * 3 // 4)
    for s, copy in enumerate(low_copies, 1):
        copy.wait_recv()
        total = total + low_in[s]
    low_all[me] = (adapter_scale_factor * total).astype(jnp.bfloat16)

    member_copies = []
    for s in range(members - 1, 0, -1):
        peer = flip(me, s)
        member_copies.append(pltpu.make_async_remote_copy(
            src_ref=low_all.at[me], dst_ref=low_all.at[me], send_sem=m_send.at[s], recv_sem=m_recv.at[s],
            device_id={"mp": peer // nrep, "rep": peer % nrep}, device_id_type=MESH))
        member_copies[-1].start()
    frozen(last, tiles * 3 // 4, tiles)
    for copy in member_copies:
        copy.wait_recv()
    a_copy.wait()

    low_t = low_all[...].astype(jnp.float32).reshape(members * rank_part, tokens)
    low_rows[...] = low_t.T.astype(jnp.bfloat16)

    def block_sum(block):
        rows = pl.ds(pl.multiple_of(block * PAD, PAD), PAD)
        low_term = jnp.dot(low_rows[rows, :], a[...], preferred_element_type=jnp.float32)
        return acc[rows, :] + low_term

    groups = d_part // 128
    out_copies = []
    for s in z_order:
        dest = flip(z, s)
        value = block_sum(dest)
        largest = jnp.abs(value[:, :128])
        for i in range(1, groups):
            largest = jnp.maximum(largest, jnp.abs(value[:, i * 128:(i + 1) * 128]))
        largest = jnp.max(largest.reshape(PAD // 8, 8, 128), axis=0)
        largest = jnp.maximum(largest, 1e-33)
        scale_out[s] = largest * (1.0 / 32767.0)
        inverse = jnp.tile(32767.0 / largest, (PAD // 8, 1))
        for i in range(groups):
            q = jnp.round(value[:, i * 128:(i + 1) * 128] * inverse)
            quant_out[s, :, i * 128:(i + 1) * 128] = q.astype(jnp.int32).astype(jnp.int16)
        for src, dst, send, recv in ((quant_out, quant_in, q_send, q_recv), (scale_out, scale_in, c_send, c_recv)):
            copy = pltpu.make_async_remote_copy(
                src_ref=src.at[s], dst_ref=dst.at[s], send_sem=send.at[s], recv_sem=recv.at[s],
                device_id={"seq": dest}, device_id_type=MESH)
            copy.start()
            out_copies.append(copy)

    rows = pl.ds(pl.multiple_of(z * PAD, PAD), PAD)
    acc[rows, :] = block_sum(z)
    for copy in out_copies:
        copy.wait_recv()
    scales = {s: jnp.tile(scale_in[s], (PAD // 8, 1)) for s in z_order}
    for i in range(groups):
        columns = slice(i * 128, (i + 1) * 128)
        result = acc[rows, columns]
        for s in z_order:
            result = result + quant_in[s, :, columns].astype(jnp.int32).astype(jnp.float32) * scales[s]
        out_ref[:, columns] = result[:TOK_DEV].astype(jnp.bfloat16)

    for copy in [*b_copies.values(), *across.values(), *beside.values(), *low_copies, *member_copies, *out_copies]:
        copy.wait_send()


def on_device(ns, nmp, nrep, grad_hidden, w_up, pool_a, pool_b, seg_adapter, adapter_slot, seg_len):
    members = nmp * nrep
    d_part, hidden = w_up.shape
    rank_part = R // members
    tokens = ns * PAD
    hbm = pl.BlockSpec(memory_space=pl.ANY)
    smem = pl.BlockSpec(memory_space=pltpu.SMEM)
    dma = pltpu.SemaphoreType.DMA
    bf16, f32 = jnp.bfloat16, jnp.float32
    scratch = [
        pltpu.VMEM(grad_hidden.shape, bf16),
        pltpu.VMEM((members, ns // members, PAD, hidden), bf16),
        pltpu.VMEM(w_up.shape, bf16),
        pltpu.VMEM((R, d_part), bf16),
        pltpu.VMEM((ns, rank_part, hidden), bf16),
        pltpu.VMEM((tokens, d_part), f32),
        pltpu.VMEM((ns, rank_part, tokens), f32),
        pltpu.VMEM((ns, rank_part, tokens), f32),
        pltpu.VMEM((members, rank_part, tokens), bf16),
        pltpu.VMEM((tokens, R), bf16),
        pltpu.VMEM((ns, PAD, d_part), jnp.int16),
        pltpu.VMEM((ns, PAD, d_part), jnp.int16),
        pltpu.VMEM((ns, 8, 128), f32),
        pltpu.VMEM((ns, 8, 128), f32),
        dma, dma((d_part // D_TILE,)), dma, dma,
        dma((nmp, K_CHUNKS)), dma((nmp, K_CHUNKS)), dma((nmp, K_CHUNKS)), dma((nmp, K_CHUNKS)),
        dma((ns,)), dma((ns,)),
        dma((ns,)), dma((ns,)), dma((members,)), dma((members,)),
        dma((ns,)), dma((ns,)), dma((ns,)), dma((ns,)),
    ]
    return pl.pallas_call(
        functools.partial(kernel, ns, nmp, nrep),
        out_shape=jax.ShapeDtypeStruct((TOK_DEV, d_part), bf16),
        in_specs=[hbm] * 4 + [smem] * 3,
        out_specs=pl.BlockSpec(memory_space=pltpu.VMEM),
        scratch_shapes=scratch,
        compiler_params=pltpu.CompilerParams(
            collective_id=0, has_side_effects=True, vmem_limit_bytes=56 * 1024 * 1024
        ),
        cost_estimate=pl.CostEstimate(
            flops=2 * tokens * d_part * hidden, bytes_accessed=2 * d_part * hidden, transcendentals=0
        ),
    )(grad_hidden, w_up, jnp.swapaxes(pool_a, 1, 2), pool_b, seg_adapter.T, adapter_slot, seg_len.T)


def solution(mesh):
    ns, nmp, nrep = mesh.shape["seq"], mesh.shape["mp"], mesh.shape["rep"]
    in_specs = (
        P(("groups", "mp", "rep"), "seq"),
        P(("mp", "rep"), "seq"),
        P(("groups", "seq"), ("mp", "rep"), None),
        P(("groups", "seq"), None, None),
        P("groups", None),
        P("groups"),
        P("groups", None),
    )
    out_specs = P(("groups", "seq"), ("mp", "rep"))
    return jax.shard_map(
        functools.partial(on_device, ns, nmp, nrep),
        mesh=mesh, in_specs=in_specs, out_specs=out_specs, check_vma=False,
    )
```

```python
import functools

import jax
import jax.numpy as jnp
from jax import lax
from jax.experimental import pallas as pl
from jax.experimental.pallas import tpu as pltpu
from jax.sharding import PartitionSpec as P

R = 64
TOK_DEV = 30
SEG = 15
PAD = 32
K_CHUNKS = 2
D_TILE = 256
MESH = pl.DeviceIdType.MESH

adapter_scale_factor = 0.5
NT = (((1,), (1,)), ((), ()))


def flip(index, bits):
    result, bit = index, 1
    while bit <= bits:
        if bits & bit:
            result = result + bit - 2 * bit * ((index // bit) % 2)
        bit *= 2
    return result


def kernel(
    ns, nmp, nrep,
    grad_hbm, w_hbm, a_hbm, b_hbm, adapter_ref, slot_ref, len_ref,
    out_ref,
    own_raw, g, w, a, b, acc, low_out, low_in, low_all, low_rows, quant_out, quant_in, scale_out, scale_in,
    own_sem, w_sem, a_sem, b_own_sem,
    gx_send, gx_recv, gs_send, gs_recv, b_send, b_recv,
    l_send, l_recv, m_send, m_recv, q_send, q_recv, c_send, c_recv,
):
    z, x, c = lax.axis_index("seq"), lax.axis_index("mp"), lax.axis_index("rep")
    members = nmp * nrep
    me = x * nrep + c
    blocks = ns
    per_dev = blocks // members
    rank_part = b.shape[1]
    hidden = w.shape[1]
    chunk = hidden // K_CHUNKS
    d_part = w.shape[0]
    tokens = blocks * PAD
    z_order = list(range(ns - 1, 0, -1))
    if ns == 4:
        z_order = [2, 3, 1]

    own_copy = pltpu.make_async_copy(grad_hbm, own_raw, own_sem)
    own_copy.start()

    barrier = pltpu.get_barrier_semaphore()
    for s in z_order:
        pl.semaphore_signal(barrier, inc=1, device_id={"seq": flip(z, s)}, device_id_type=MESH)
    for s in range(1, members):
        peer = flip(me, s)
        pl.semaphore_signal(
            barrier, inc=1, device_id={"mp": peer // nrep, "rep": peer % nrep}, device_id_type=MESH
        )

    def w_copy(t):
        rows = pl.ds(pl.multiple_of(t * D_TILE, D_TILE), D_TILE)
        return pltpu.make_async_copy(w_hbm.at[rows], w.at[rows], w_sem.at[t])

    tiles = d_part // D_TILE
    a_copy = pltpu.make_async_copy(a_hbm.at[0], a, a_sem)

    pl.semaphore_wait(barrier, ns - 1 + members - 1)

    def b_part(q):
        return b_hbm.at[0, pl.ds(pl.multiple_of(me * rank_part, rank_part), rank_part),
                        pl.ds(pl.multiple_of(q * hidden, hidden), hidden)]

    b_copies = {}
    for s in z_order:
        b_copies[s] = pltpu.make_async_remote_copy(
            src_ref=b_part(flip(z, s)), dst_ref=b.at[s],
            send_sem=b_send.at[s], recv_sem=b_recv.at[s],
            device_id={"seq": flip(z, s)}, device_id_type=MESH)
        b_copies[s].start()

    own_copy.wait()
    row = lax.broadcasted_iota(jnp.int32, (TOK_DEV, 1), 0)
    second = row >= SEG
    for i in range(per_dev):
        block = me * per_dev + i
        length = jnp.where(second, len_ref[1, block] + SEG, len_ref[0, block])
        rows = own_raw[i * TOK_DEV:(i + 1) * TOK_DEV, :]
        rows = jnp.where(row < length, rows.astype(jnp.float32), 0.0).astype(jnp.bfloat16)
        rows = jnp.concatenate([rows, jnp.zeros((PAD - TOK_DEV, hidden), jnp.bfloat16)], axis=0)
        g[me, i] = rows

    def g_part(member, k):
        return g.at[member, :, :, k * chunk:(k + 1) * chunk]

    def g_copy(member, k, send, recv, s, device):
        return pltpu.make_async_remote_copy(
            src_ref=g_part(member, k), dst_ref=g_part(member, k),
            send_sem=send.at[s, k], recv_sem=recv.at[s, k],
            device_id=device, device_id_type=MESH)

    across, beside = {}, {}
    sibling = {"rep": flip(c, 1)}
    for k in range(K_CHUNKS):
        for s in range(1, nmp):
            across[s, k] = g_copy(me, k, gx_send, gx_recv, s, {"mp": flip(x, s)})
            across[s, k].start()
        beside[0, k] = g_copy(me, k, gs_send, gs_recv, 0, sibling)
        beside[0, k].start()
    b_own = pltpu.make_async_copy(b_part(z), b.at[0], b_own_sem)
    b_own.start()
    for t in range(tiles):
        w_copy(t).start()
    a_copy.start()

    def frozen(k, first, last):
        def tile_step(t, carry):
            rows = pl.ds(pl.multiple_of(t * D_TILE, D_TILE), D_TILE)
            if k == 0:
                w_copy(t).wait()
            part = lax.dot_general(
                g[:, :, :, k * chunk:(k + 1) * chunk].reshape(tokens, chunk),
                w[rows, k * chunk:(k + 1) * chunk], NT,
                preferred_element_type=jnp.float32)
            if k == 0:
                acc[:, rows] = part
            else:
                acc[:, rows] += part
            return carry

        lax.fori_loop(first, last, tile_step, 0)

    for k in range(K_CHUNKS):
        for s in range(1, nmp):
            across[s, k].wait_recv()
            beside[s, k] = g_copy(flip(x, s) * nrep + c, k, gs_send, gs_recv, s, sibling)
            beside[s, k].start()
        for s in range(nmp):
            beside[s, k].wait_recv()
        if k < K_CHUNKS - 1:
            frozen(k, 0, tiles)

    lane = lax.broadcasted_iota(jnp.int32, (1, tokens), 1)
    slots = jnp.zeros((1, tokens), jnp.int32)
    for block in range(blocks):
        for j in range(2):
            slot = slot_ref[adapter_ref[j, block]]
            slots = jnp.where(lane >= block * PAD + j * SEG, slot, slots)

    def low_part(s):
        every = lax.dot_general(
            b[s], g[...].reshape(tokens, hidden), NT, preferred_element_type=jnp.float32)
        return jnp.where(slots == flip(z, s), every, 0.0)

    b_own.wait()
    total = low_part(0)
    last = K_CHUNKS - 1
    low_copies = []
    for s in range(1, ns):
        if s == min(2, ns - 1):
            frozen(last, 0, tiles // 4)
        b_copies[s].wait_recv()
        low_out[s] = low_part(s)
        low_copies.append(pltpu.make_async_remote_copy(
            src_ref=low_out.at[s], dst_ref=low_in.at[s], send_sem=l_send.at[s], recv_sem=l_recv.at[s],
            device_id={"seq": flip(z, s)}, device_id_type=MESH))
        low_copies[-1].start()
    frozen(last, tiles // 4, tiles * 5 // 8)
    for s, copy in enumerate(low_copies, 1):
        copy.wait_recv()
        total = total + low_in[s]
    low_all[me] = (adapter_scale_factor * total).astype(jnp.bfloat16)

    member_copies = []
    for s in range(members - 1, 0, -1):
        peer = flip(me, s)
        member_copies.append(pltpu.make_async_remote_copy(
            src_ref=low_all.at[me], dst_ref=low_all.at[me], send_sem=m_send.at[s], recv_sem=m_recv.at[s],
            device_id={"mp": peer // nrep, "rep": peer % nrep}, device_id_type=MESH))
        member_copies[-1].start()
    frozen(last, tiles * 5 // 8, tiles)
    for copy in member_copies:
        copy.wait_recv()
    a_copy.wait()

    low_t = low_all[...].astype(jnp.float32).reshape(members * rank_part, tokens)
    low_rows[...] = low_t.T.astype(jnp.bfloat16)

    def block_sum(block):
        rows = pl.ds(pl.multiple_of(block * PAD, PAD), PAD)
        low_term = jnp.dot(low_rows[rows, :], a[...], preferred_element_type=jnp.float32)
        return acc[rows, :] + low_term

    groups = d_part // 128
    out_copies = []
    for s in z_order:
        dest = flip(z, s)
        value = block_sum(dest)
        largest = jnp.abs(value[:, :128])
        for i in range(1, groups):
            largest = jnp.maximum(largest, jnp.abs(value[:, i * 128:(i + 1) * 128]))
        largest = jnp.max(largest.reshape(PAD // 8, 8, 128), axis=0)
        largest = jnp.maximum(largest, 1e-33)
        scale_out[s] = largest * (1.0 / 32767.0)
        inverse = jnp.tile(32767.0 / largest, (PAD // 8, 1))
        for i in range(groups):
            q = jnp.round(value[:, i * 128:(i + 1) * 128] * inverse)
            quant_out[s, :, i * 128:(i + 1) * 128] = q.astype(jnp.int32).astype(jnp.int16)
        for src, dst, send, recv in ((quant_out, quant_in, q_send, q_recv), (scale_out, scale_in, c_send, c_recv)):
            copy = pltpu.make_async_remote_copy(
                src_ref=src.at[s], dst_ref=dst.at[s], send_sem=send.at[s], recv_sem=recv.at[s],
                device_id={"seq": dest}, device_id_type=MESH)
            copy.start()
            out_copies.append(copy)

    rows = pl.ds(pl.multiple_of(z * PAD, PAD), PAD)
    acc[rows, :] = block_sum(z)
    for copy in out_copies:
        copy.wait_recv()
    scales = {s: jnp.tile(scale_in[s], (PAD // 8, 1)) for s in z_order}
    for i in range(groups):
        columns = slice(i * 128, (i + 1) * 128)
        result = acc[rows, columns]
        for s in z_order:
            result = result + quant_in[s, :, columns].astype(jnp.int32).astype(jnp.float32) * scales[s]
        out_ref[:, columns] = result[:TOK_DEV].astype(jnp.bfloat16)

    for copy in [*b_copies.values(), *across.values(), *beside.values(), *low_copies, *member_copies, *out_copies]:
        copy.wait_send()


def on_device(ns, nmp, nrep, grad_hidden, w_up, pool_a, pool_b, seg_adapter, adapter_slot, seg_len):
    members = nmp * nrep
    d_part, hidden = w_up.shape
    rank_part = R // members
    tokens = ns * PAD
    hbm = pl.BlockSpec(memory_space=pl.ANY)
    smem = pl.BlockSpec(memory_space=pltpu.SMEM)
    dma = pltpu.SemaphoreType.DMA
    bf16, f32 = jnp.bfloat16, jnp.float32
    scratch = [
        pltpu.VMEM(grad_hidden.shape, bf16),
        pltpu.VMEM((members, ns // members, PAD, hidden), bf16),
        pltpu.VMEM(w_up.shape, bf16),
        pltpu.VMEM((R, d_part), bf16),
        pltpu.VMEM((ns, rank_part, hidden), bf16),
        pltpu.VMEM((tokens, d_part), f32),
        pltpu.VMEM((ns, rank_part, tokens), f32),
        pltpu.VMEM((ns, rank_part, tokens), f32),
        pltpu.VMEM((members, rank_part, tokens), bf16),
        pltpu.VMEM((tokens, R), bf16),
        pltpu.VMEM((ns, PAD, d_part), jnp.int16),
        pltpu.VMEM((ns, PAD, d_part), jnp.int16),
        pltpu.VMEM((ns, 8, 128), f32),
        pltpu.VMEM((ns, 8, 128), f32),
        dma, dma((d_part // D_TILE,)), dma, dma,
        dma((nmp, K_CHUNKS)), dma((nmp, K_CHUNKS)), dma((nmp, K_CHUNKS)), dma((nmp, K_CHUNKS)),
        dma((ns,)), dma((ns,)),
        dma((ns,)), dma((ns,)), dma((members,)), dma((members,)),
        dma((ns,)), dma((ns,)), dma((ns,)), dma((ns,)),
    ]
    return pl.pallas_call(
        functools.partial(kernel, ns, nmp, nrep),
        out_shape=jax.ShapeDtypeStruct((TOK_DEV, d_part), bf16),
        in_specs=[hbm] * 4 + [smem] * 3,
        out_specs=pl.BlockSpec(memory_space=pltpu.VMEM),
        scratch_shapes=scratch,
        compiler_params=pltpu.CompilerParams(
            collective_id=0, has_side_effects=True, vmem_limit_bytes=56 * 1024 * 1024
        ),
        cost_estimate=pl.CostEstimate(
            flops=2 * tokens * d_part * hidden, bytes_accessed=2 * d_part * hidden, transcendentals=0
        ),
    )(grad_hidden, w_up, jnp.swapaxes(pool_a, 1, 2), pool_b, seg_adapter.T, adapter_slot, seg_len.T)


def solution(mesh):
    ns, nmp, nrep = mesh.shape["seq"], mesh.shape["mp"], mesh.shape["rep"]
    in_specs = (
        P(("groups", "mp", "rep"), "seq"),
        P(("mp", "rep"), "seq"),
        P(("groups", "seq"), ("mp", "rep"), None),
        P(("groups", "seq"), None, None),
        P("groups", None),
        P("groups"),
        P("groups", None),
    )
    out_specs = P(("groups", "seq"), ("mp", "rep"))
    return jax.shard_map(
        functools.partial(on_device, ns, nmp, nrep),
        mesh=mesh, in_specs=in_specs, out_specs=out_specs, check_vma=False,
    )
```
